32 devices in a mesh: sec: 2 (over y), row: 4 (over x, core), col: 4 (over z).
Axes of the slice: x: 2, y: 2, z: 4, core: 2. Of those that a mesh axis runs over, the one named last changes fastest.
Arguments:
- sketch: float32 [32, 64, 2048], P(None, ('sec', 'row'), 'col'), parts along dimension 1, may hold values from -6 to 6
- weights: float32 [8, 64, 2048], P(None, ('sec', 'row'), 'col'), parts along dimension 1, may hold values from 0.05 to 1
Outputs:
- basis: float32 [32, 64, 2048], P(None, ('sec', 'row'), 'col'), parts along dimension 1
- factor: float32 [64, 32], P('sec'), parts along dimension 0
The draws below stay inside these ranges and needn't reach their ends.
There are 2 independent parts, one for each index of `sec`. The reference program is written for one: setup_inputs(seed, part) draws one part's arguments, and reference() takes and returns one part's arrays. A program takes and returns all parts, laid end to end along the dimension named above; each array names one. Nothing has to cross between parts.
All inputs are finite; a program needn't handle non-finite values.
Results may differ from the reference program's by a relative error of at most 0.0001.
Values sent between devices are 32-bit elements; how exact they have to be, the bound alone decides.
A program may use at most 64 MiB of HBM per device.

```python
import math
import jax
import jax.numpy as jnp
from jax import lax

K = 32
ITERS = 2
H = 32
W = 2048


def steps_of(stream_key, extent, split, low, largest):
    gain, own = 1.0, jax.random.fold_in(stream_key, 6)
    for axis_at, parts in split:
        steps = jnp.exp(jax.random.uniform(jax.random.fold_in(own, axis_at), (parts,), jnp.float32, low / len(split), largest / len(split)))
        gain = gain * jnp.repeat(steps, extent[axis_at] // parts).reshape([-1 if axis == axis_at else 1 for axis in range(len(extent))])
    return gain


def scatter_about(stream_key, dims, width, bound, shards=(), kind=jnp.bfloat16):
    result = width * jax.random.normal(stream_key, dims, jnp.float32)
    if shards:
        result = result * steps_of(stream_key, dims, shards, -0.22, 0.18)
    return jnp.clip(result, -bound, bound).astype(kind)


def setup_inputs(seed: int = 0, part: int = 0) -> dict:
    key_of = jax.random.split(jax.random.key(seed), 3)
    part_splits = jax.random.split(jax.random.fold_in(key_of[2], part), 3)
    return {
        "sketch": scatter_about(part_splits[0], (K, H, W), 1.0, 6.0, ((1, 4), (2, 4)), jnp.float32),
        "weights": jnp.clip(jnp.exp(math.log(1.0) - 2.9957323 * jax.random.uniform(part_splits[1], (8, H, W), jnp.float32) ** steps_of(part_splits[1], (8, H, W), ((1, 4), (2, 4)), -0.2, 0.2)), 0.05, 1.0),
    }


NEIGHBOURS = ((-1, -1), (-1, 0), (-1, 1), (0, -1), (0, 1), (1, -1), (1, 0), (1, 1))

def operate(planes, weights):
    height = planes.shape[1]
    breadth = planes.shape[2]
    padded = jnp.pad(planes, ((0, 0), (1, 1), (1, 1)))
    summed = jnp.sum(weights, axis=0) * planes
    for position, offset in enumerate(NEIGHBOURS):
        shift_row = offset[0]
        shift_col = offset[1]
        summed = summed + weights[position] * padded[:, 1 + shift_row:1 + shift_row + height, 1 + shift_col:1 + shift_col + breadth]
    return summed

def reference(sketch, weights):
    sketch_field = sketch
    lower_tri = jnp.zeros((K, K), jnp.float32)
    for power_step in range(ITERS):
        blocks = sketch_field.reshape(K // 8, 8, H, W)
        image_vals = lax.map(lambda block: operate(block, weights), blocks).reshape(K, H * W)
        gram_full = jnp.dot(image_vals, image_vals.T, precision=lax.Precision.HIGHEST) / (H * W)
        lower_tri = jnp.linalg.cholesky(gram_full)
        solved = jax.scipy.linalg.solve_triangular(lower_tri, image_vals, lower=True)
        sketch_field = solved.reshape(K, H, W)
    return (sketch_field, lower_tri.T)
```

```python
import functools

import jax
import jax.numpy as jnp
from jax import lax
from jax.experimental import pallas as pl
from jax.experimental.pallas import tpu as pltpu
from jax.sharding import PartitionSpec as P

LANES = 128
SUB = 8
NEIGHBOURS = ((-1, -1), (-1, 0), (-1, 1), (0, -1), (0, 1), (1, -1), (1, 0), (1, 1))
MESH = pl.DeviceIdType.MESH
NT = (((1,), (1,)), ((), ()))
HIGHEST = lax.Precision.HIGHEST


def split(x):
    hi = x.astype(jnp.bfloat16)
    lo = (x - hi.astype(jnp.float32)).astype(jnp.bfloat16)
    return hi, lo


def kernel(
    n, rows, cols, R, C,
    sk_hbm, w_hbm, out_ref, fac_ref,
    raw, wraw, staged, ext, y1, y2, pack, nb, gr, gc, gsend1, gsend2,
    load_sem, store_sem, row_send, row_recv, nb_send, nb_recv, gr_send, gr_recv, gc_send, gc_recv,
):
    groups = n // SUB
    all_groups = groups + 1
    wide = cols + LANES
    i = lax.axis_index("row")
    j = lax.axis_index("col")
    has_up, has_down = i > 0, i < R - 1
    has_left, has_right = j > 0, j < C - 1

    tiles = cols // LANES
    loads = []
    for t in range(tiles):
        across = pl.ds(t * LANES, LANES)
        loads.append(pltpu.make_async_copy(sk_hbm.at[:, across], raw.at[t], load_sem.at[0, t]))
        loads.append(pltpu.make_async_copy(w_hbm.at[:, across], wraw.at[t], load_sem.at[1, t]))
    for load in loads:
        load.start()

    barrier = pltpu.get_barrier_semaphore()
    for d in range(1, R):
        pl.semaphore_signal(
            barrier, inc=1, device_id={"row": lax.rem(i + d, R), "col": j}, device_id_type=MESH
        )
    for d in range(1, C):
        pl.semaphore_signal(
            barrier, inc=1, device_id={"row": i, "col": lax.rem(j + d, C)}, device_id_type=MESH
        )
    ups = ((-1, has_up), (0, None), (1, has_down))
    sides = ((-1, has_left), (1, has_right))
    for dr, ok_r in ups:
        for dc, ok_c in sides:
            if dr != 0:
                @pl.when(jnp.logical_and(ok_r, ok_c))
                def _(dr=dr, dc=dc):
                    pl.semaphore_signal(
                        barrier, inc=1, device_id={"row": i + dr, "col": j + dc},
                        device_id_type=MESH,
                    )
    diagonals = (has_up.astype(jnp.int32) + has_down.astype(jnp.int32)) * (
        has_left.astype(jnp.int32) + has_right.astype(jnp.int32)
    )

    lane = lax.broadcasted_iota(jnp.int32, (SUB, LANES), 1)

    def relayout(r):
        for t in range(tiles):
            across = slice(t * LANES, (t + 1) * LANES)
            for g in range(groups):
                ext[r + 2, g * SUB : (g + 1) * SUB, across] = raw[
                    t, pl.ds(g * SUB * rows + r, SUB, stride=rows), :
                ]
            ext[r + 2, n : n + SUB, across] = wraw[t, pl.ds(r, SUB, stride=rows), :]

    for load in loads:
        load.wait()
    for r in range(rows):
        relayout(r)

    packed = [jnp.zeros((SUB, LANES), jnp.float32), jnp.zeros((SUB, LANES), jnp.float32)]
    for r in range(rows):
        for g in range(all_groups):
            which, slot = (0, r * groups + g) if g < groups else (1, r)
            edge = jnp.where(
                lane < LANES // 2,
                ext[r + 2, g * SUB : (g + 1) * SUB, 0:LANES],
                ext[r + 2, g * SUB : (g + 1) * SUB, cols - LANES : cols],
            )
            moved = pltpu.roll(edge, (4 * slot + 2) % LANES, 1)
            packed[which] = jnp.where(lane // 4 == slot, moved, packed[which])
    pack[0:SUB, :] = packed[0]
    pack[SUB : 2 * SUB, :] = packed[1]

    pl.semaphore_wait(barrier, (R - 1) + (C - 1) + diagonals)

    def edge_copy(dr, dc):
        at = (1 - dr) * 2 + (0 if dc > 0 else 1)
        return pltpu.make_async_remote_copy(
            src_ref=pack, dst_ref=nb.at[at], send_sem=nb_send.at[at], recv_sem=nb_recv.at[at],
            device_id={"row": i + dr, "col": j + dc}, device_id_type=MESH,
        )

    def cond(*terms):
        terms = [t for t in terms if t is not None]
        return functools.reduce(jnp.logical_and, terms)

    def row_copy(down):
        src = rows if down else 2
        dst = 0 if down else rows + 2
        at = 0 if down else 1
        return pltpu.make_async_remote_copy(
            src_ref=ext.at[pl.ds(src, 2), :, pl.ds(0, cols)],
            dst_ref=ext.at[pl.ds(dst, 2), :, pl.ds(0, cols)],
            send_sem=row_send.at[at], recv_sem=row_recv.at[at],
            device_id={"row": i + (1 if down else -1), "col": j}, device_id_type=MESH,
        )

    for dr, ok_r in ups:
        for dc, ok_c in sides:
            @pl.when(cond(ok_r, ok_c))
            def _(dr=dr, dc=dc):
                edge_copy(dr, dc).start()

    @pl.when(has_down)
    def _():
        row_copy(True).start()

    @pl.when(has_up)
    def _():
        row_copy(False).start()

    @pl.when(jnp.logical_not(has_up))
    def _():
        ext[0:2, :, 0:cols] = jnp.zeros((2, n + SUB, cols), jnp.float32)

    @pl.when(jnp.logical_not(has_down))
    def _():
        ext[rows + 2 : rows + 4, :, 0:cols] = jnp.zeros((2, n + SUB, cols), jnp.float32)

    for dr, ok_r in ups:
        for dc, ok_c in sides:
            at = (1 + dr) * 2 + (1 if dc > 0 else 0)
            ok = cond(ok_r, ok_c)

            @pl.when(jnp.logical_not(ok))
            def _(at=at):
                nb[at] = jnp.zeros((2 * SUB, LANES), jnp.float32)

            @pl.when(ok)
            def _(dr=dr, dc=dc):
                edge_copy(-dr, -dc).wait_recv()

    for dr in (0, -1, 1):
        at = (1 + dr) * 2
        merged = [
            jnp.where(
                lane % 4 < 2,
                nb[at, h * SUB : (h + 1) * SUB, :],
                nb[at + 1, h * SUB : (h + 1) * SUB, :],
            )
            for h in range(2)
        ]
        pairs = {
            0: [(r + 2, r) for r in range(rows)],
            -1: [(0, rows - 2), (1, rows - 1)],
            1: [(rows + 2, 0), (rows + 3, 1)],
        }[dr]
        for e, r in pairs:
            for g in range(all_groups):
                which, slot = (0, r * groups + g) if g < groups else (1, r)
                ext[e, g * SUB : (g + 1) * SUB, cols:wide] = pltpu.roll(
                    merged[which], (-(4 * slot + 2)) % LANES, 1
                )

    @pl.when(has_up)
    def _():
        row_copy(True).wait_recv()

    @pl.when(has_down)
    def _():
        row_copy(False).wait_recv()

    def apply(src, e, e_w, g, width):
        at = pl.ds(g * SUB, SUB)
        parts = {}
        for a in (-1, 0, 1):
            v = src[e + a, at, :]
            parts[a, 0] = v[:, :width]
            parts[a, -1] = pltpu.roll(v, 1, 1)[:, :width]
            parts[a, 1] = pltpu.roll(v, wide - 1, 1)[:, :width]
        taps = [
            jnp.broadcast_to(ext[e_w, pl.ds(n + k, 1), 0:width], (SUB, width)) for k in range(SUB)
        ]
        total = functools.reduce(jnp.add, taps) * parts[0, 0]
        for k, offset in enumerate(NEIGHBOURS):
            total = total + taps[k] * parts[offset]
        return total

    def first(e, carry):
        for g in range(groups):
            y1[e - 1, g * SUB : (g + 1) * SUB, :] = apply(ext, e, e, g, wide)
        return carry

    lax.fori_loop(1, rows + 3, first, 0)

    def second(r, carry):
        for g in range(groups):
            y2[r, g * SUB : (g + 1) * SUB, :] = apply(y1, r + 1, r + 2, g, cols)
        return carry

    lax.fori_loop(0, rows, second, 0)

    def gram(load):
        total = jnp.zeros((2 * n, 2 * n), jnp.float32)
        for r in range(rows):
            both = jnp.concatenate(split(load(r)), axis=0)
            total = total + lax.dot_general(both, both, NT, preferred_element_type=jnp.float32)
        half = total[0:n] + total[n : 2 * n]
        return half[:, 0:n] + half[:, n : 2 * n]

    gram_1 = gram(lambda r: y1[r + 1, :, 0:cols])
    gram_2 = gram(lambda r: y2[r])
    grams = jnp.concatenate([gram_1, gram_2], axis=1) * (1.0 / (rows * cols * R * C))
    compact = jnp.concatenate([grams[0 : n // 2], grams[n // 2 : n]], axis=1)

    def exchange(value, sent, held, me, count, axis, send_sems, recv_sems):
        sent[...] = value
        held[me] = value

        def target(d):
            peer = lax.rem(me + d, count)
            return {"row": peer, "col": j} if axis == "row" else {"row": i, "col": peer}

        copies = [
            pltpu.make_async_remote_copy(
                src_ref=sent, dst_ref=held.at[me], send_sem=send_sems.at[d - 1],
                recv_sem=recv_sems.at[me], device_id=target(d), device_id_type=MESH,
            )
            for d in range(1, count)
        ]
        for copy in copies:
            copy.start()
        for d in range(1, count):
            peer = lax.rem(me + d, count)
            pltpu.make_async_remote_copy(
                src_ref=sent, dst_ref=held.at[peer], send_sem=send_sems.at[d - 1],
                recv_sem=recv_sems.at[peer], device_id=target(d), device_id_type=MESH,
            ).wait_recv()
        total = held[0]
        for at in range(1, count):
            total = total + held[at]
        return total, copies

    in_row, row_copies = exchange(compact, gsend1, gr, i, R, "row", gr_send, gr_recv)
    in_all, col_copies = exchange(in_row, gsend2, gc, j, C, "col", gc_send, gc_recv)

    whole = jnp.concatenate([in_all, pltpu.roll(in_all, LANES // 2, 1)], axis=0)
    later = pltpu.roll(whole, n, 1)
    sub_n = lax.broadcasted_iota(jnp.int32, (n, LANES), 0)
    lane_n = lax.broadcasted_iota(jnp.int32, (n, LANES), 1)
    quarter = lane_n // n
    eye = (lane_n % n == sub_n).astype(jnp.float32)
    table = jnp.where(quarter == 0, whole, jnp.where(quarter == 2, later, eye))
    blocks = [table[g * SUB : (g + 1) * SUB] for g in range(groups)]
    sub = lax.broadcasted_iota(jnp.int32, (SUB, LANES), 0)
    low_half = lane < LANES // 2
    for p in range(n):
        home = p // SUB
        row = jnp.broadcast_to(blocks[home][p % SUB : p % SUB + 1, :], (SUB, LANES))
        pivot = jnp.where(low_half, row[:, p : p + 1], row[:, 2 * n + p : 2 * n + p + 1])
        scaled = row / pivot
        for g in range(home, groups):
            mine = blocks[g]
            factor = jnp.where(low_half, mine[:, p : p + 1], mine[:, 2 * n + p : 2 * n + p + 1])
            update = factor * scaled
            if g == home:
                update = jnp.where(sub > p % SUB, update, 0.0)
            blocks[g] = mine - update
    table = jnp.concatenate(blocks, axis=0)
    on_diagonal = lane_n % n == sub_n
    diag_1 = jnp.sum(
        jnp.where(jnp.logical_and(on_diagonal, quarter == 0), table, 0.0), axis=1, keepdims=True
    )
    diag_2 = jnp.sum(
        jnp.where(jnp.logical_and(on_diagonal, quarter == 2), table, 0.0), axis=1, keepdims=True
    )
    table = table / jnp.sqrt(jnp.where(quarter < 2, diag_1, diag_2))
    inverse_1 = table[:, n : 2 * n]
    upper_2 = table[:, 2 * n : 3 * n]
    inverse_2 = table[:, 3 * n : 4 * n]
    row_at = lax.broadcasted_iota(jnp.int32, (n, n), 0)
    col_at = lax.broadcasted_iota(jnp.int32, (n, n), 1)
    upper_2 = jnp.where(col_at >= row_at, upper_2, 0.0)
    last = lax.dot_general(
        upper_2, inverse_1, NT, precision=HIGHEST, preferred_element_type=jnp.float32
    )
    fac_ref[...] = jnp.where(col_at >= row_at, last, 0.0)

    inv_hi, inv_lo = split(inverse_2)
    left = jnp.concatenate([inv_hi, inv_lo, inv_hi], axis=1)
    stores = []
    for t0 in range(0, tiles, 2):
        for r in range(rows):
            hi, lo = split(y2[r, :, t0 * LANES : (t0 + 2) * LANES])
            right = jnp.concatenate([hi, hi, lo], axis=0)
            solved = jnp.dot(left, right, preferred_element_type=jnp.float32)
            for t in range(2):
                for g in range(groups):
                    staged[t0 + t, pl.ds(g * SUB * rows + r, SUB, stride=rows), :] = solved[
                        g * SUB : (g + 1) * SUB, t * LANES : (t + 1) * LANES
                    ]
        for t in range(t0, t0 + 2):
            stores.append(pltpu.make_async_copy(
                staged.at[t], out_ref.at[:, pl.ds(t * LANES, LANES)], store_sem.at[t]
            ))
            stores[-1].start()
    for store in stores:
        store.wait()

    for dr, ok_r in ups:
        for dc, ok_c in sides:
            @pl.when(cond(ok_r, ok_c))
            def _(dr=dr, dc=dc):
                edge_copy(dr, dc).wait_send()

    @pl.when(has_down)
    def _():
        row_copy(True).wait_send()

    @pl.when(has_up)
    def _():
        row_copy(False).wait_send()

    for copy in row_copies + col_copies:
        copy.wait_send()


def on_device(sketch, weights):
    n, rows, cols = sketch.shape
    R, C = lax.axis_size("row"), lax.axis_size("col")
    dma = pltpu.SemaphoreType.DMA
    f32 = jnp.float32
    basis, factor = pl.pallas_call(
        functools.partial(kernel, n, rows, cols, R, C),
        out_shape=(
            jax.ShapeDtypeStruct((n * rows, cols), f32),
            jax.ShapeDtypeStruct((n, n), f32),
        ),
        in_specs=[pl.BlockSpec(memory_space=pl.ANY)] * 2,
        out_specs=(
            pl.BlockSpec(memory_space=pl.ANY),
            pl.BlockSpec(memory_space=pltpu.VMEM),
        ),
        scratch_shapes=[
            pltpu.VMEM((cols // LANES, n * rows, LANES), f32),
            pltpu.VMEM((cols // LANES, SUB * rows, LANES), f32),
            pltpu.VMEM((cols // LANES, n * rows, LANES), f32),
            pltpu.VMEM((rows + 4, n + SUB, cols + LANES), f32),
            pltpu.VMEM((rows + 2, n, cols + LANES), f32),
            pltpu.VMEM((rows, n, cols), f32),
            pltpu.VMEM((2 * SUB, LANES), f32),
            pltpu.VMEM((6, 2 * SUB, LANES), f32),
            pltpu.VMEM((R, n // 2, LANES), f32),
            pltpu.VMEM((C, n // 2, LANES), f32),
            pltpu.VMEM((n // 2, LANES), f32),
            pltpu.VMEM((n // 2, LANES), f32),
            dma((2, cols // LANES)), dma((cols // LANES,)), dma((2,)), dma((2,)), dma((6,)), dma((6,)),
            dma((R,)), dma((R,)), dma((C,)), dma((C,)),
        ],
        compiler_params=pltpu.CompilerParams(
            collective_id=0, has_side_effects=True, vmem_limit_bytes=32 * 1024 * 1024
        ),
    )(sketch.reshape(n * rows, cols), weights.reshape(SUB * rows, cols))
    return basis.reshape(n, rows, cols), factor


def solution(mesh):
    return jax.shard_map(
        on_device,
        mesh=mesh,
        in_specs=(P(None, ("sec", "row"), "col"), P(None, ("sec", "row"), "col")),
        out_specs=(P(None, ("sec", "row"), "col"), P("sec", None)),
        check_vma=False,
    )
```

```python
import functools

import jax
import jax.numpy as jnp
from jax import lax
from jax.experimental import pallas as pl
from jax.experimental.pallas import tpu as pltpu
from jax.sharding import PartitionSpec as P

LANES = 128
SUB = 8
NEIGHBOURS = ((-1, -1), (-1, 0), (-1, 1), (0, -1), (0, 1), (1, -1), (1, 0), (1, 1))
MESH = pl.DeviceIdType.MESH
NT = (((1,), (1,)), ((), ()))
HIGHEST = lax.Precision.HIGHEST


def split(x):
    hi = x.astype(jnp.bfloat16)
    lo = (x - hi.astype(jnp.float32)).astype(jnp.bfloat16)
    return hi, lo


def kernel(
    n, rows, cols, R, C,
    sk_hbm, w_hbm, out_ref, fac_ref,
    raw, wraw, staged, ext, ext_l, ext_r, y1, y1_l, y1_r, y2, pack, nb, held_row, held_col, sent,
    load_sem, store_sem, row_send, row_recv, nb_send, nb_recv, gr_send, gr_recv, gc_send, gc_recv,
):
    groups = n // SUB
    all_groups = groups + 1
    wide = cols + LANES
    i = lax.axis_index("row")
    j = lax.axis_index("col")
    has_up, has_down = i > 0, i < R - 1
    has_left, has_right = j > 0, j < C - 1

    tiles = cols // LANES
    loads = []
    for t in range(tiles):
        across = pl.ds(t * LANES, LANES)
        loads.append(pltpu.make_async_copy(sk_hbm.at[:, across], raw.at[t], load_sem.at[0, t]))
        loads.append(pltpu.make_async_copy(w_hbm.at[:, across], wraw.at[t], load_sem.at[1, t]))
    for load in loads:
        load.start()

    barrier = pltpu.get_barrier_semaphore()
    for d in range(1, R):
        pl.semaphore_signal(
            barrier, inc=1, device_id={"row": lax.rem(i + d, R), "col": j}, device_id_type=MESH
        )
    for d in range(1, C):
        pl.semaphore_signal(
            barrier, inc=1, device_id={"row": i, "col": lax.rem(j + d, C)}, device_id_type=MESH
        )
    ups = ((-1, has_up), (0, None), (1, has_down))
    sides = ((-1, has_left), (1, has_right))
    for dr, ok_r in ups:
        for dc, ok_c in sides:
            if dr != 0:
                @pl.when(jnp.logical_and(ok_r, ok_c))
                def _(dr=dr, dc=dc):
                    pl.semaphore_signal(
                        barrier, inc=1, device_id={"row": i + dr, "col": j + dc},
                        device_id_type=MESH,
                    )
    diagonals = (has_up.astype(jnp.int32) + has_down.astype(jnp.int32)) * (
        has_left.astype(jnp.int32) + has_right.astype(jnp.int32)
    )

    lane = lax.broadcasted_iota(jnp.int32, (SUB, LANES), 1)

    def relayout(r):
        for t in range(tiles):
            across = slice(t * LANES, (t + 1) * LANES)
            for g in range(groups):
                ext[r + 2, g * SUB : (g + 1) * SUB, across] = raw[
                    t, pl.ds(g * SUB * rows + r, SUB, stride=rows), :
                ]
            ext[r + 2, n : n + SUB, across] = wraw[t, pl.ds(r, SUB, stride=rows), :]

    for load in loads:
        load.wait()
    for r in range(rows):
        relayout(r)

    def edge_copy(dr, dc):
        at = (1 - dr) * 2 + (0 if dc > 0 else 1)
        return pltpu.make_async_remote_copy(
            src_ref=pack, dst_ref=nb.at[at], send_sem=nb_send.at[at], recv_sem=nb_recv.at[at],
            device_id={"row": i + dr, "col": j + dc}, device_id_type=MESH,
        )

    def cond(*terms):
        terms = [t for t in terms if t is not None]
        return functools.reduce(jnp.logical_and, terms)

    def row_copy(down):
        src = rows if down else 2
        dst = 0 if down else rows + 2
        at = 0 if down else 1
        return pltpu.make_async_remote_copy(
            src_ref=ext.at[pl.ds(src, 2), :, pl.ds(0, cols)],
            dst_ref=ext.at[pl.ds(dst, 2), :, pl.ds(0, cols)],
            send_sem=row_send.at[at], recv_sem=row_recv.at[at],
            device_id={"row": i + (1 if down else -1), "col": j}, device_id_type=MESH,
        )

    pl.semaphore_wait(barrier, (R - 1) + (C - 1) + diagonals)

    @pl.when(has_down)
    def _():
        row_copy(True).start()

    @pl.when(has_up)
    def _():
        row_copy(False).start()

    packed = [jnp.zeros((SUB, LANES), jnp.float32), jnp.zeros((SUB, LANES), jnp.float32)]
    for r in range(rows):
        for g in range(all_groups):
            which, slot = (0, r * groups + g) if g < groups else (1, r)
            edge = jnp.where(
                lane < LANES // 2,
                ext[r + 2, g * SUB : (g + 1) * SUB, 0:LANES],
                ext[r + 2, g * SUB : (g + 1) * SUB, cols - LANES : cols],
            )
            moved = pltpu.roll(edge, (4 * slot + 2) % LANES, 1)
            packed[which] = jnp.where(lane // 4 == slot, moved, packed[which])
    pack[0:SUB, :] = packed[0]
    pack[SUB : 2 * SUB, :] = packed[1]

    for dr, ok_r in (ups[1], ups[0], ups[2]):
        for dc, ok_c in sides:
            @pl.when(cond(ok_r, ok_c))
            def _(dr=dr, dc=dc):
                edge_copy(dr, dc).start()

    @pl.when(jnp.logical_not(has_up))
    def _():
        ext[0:2, :, 0:cols] = jnp.zeros((2, n + SUB, cols), jnp.float32)

    @pl.when(jnp.logical_not(has_down))
    def _():
        ext[rows + 2 : rows + 4, :, 0:cols] = jnp.zeros((2, n + SUB, cols), jnp.float32)

    def receive_edges(dr, ok_r):
        for dc, ok_c in sides:
            at = (1 + dr) * 2 + (1 if dc > 0 else 0)
            ok = cond(ok_r, ok_c)

            @pl.when(jnp.logical_not(ok))
            def _(at=at):
                nb[at] = jnp.zeros((2 * SUB, LANES), jnp.float32)

            @pl.when(ok)
            def _(dr=dr, dc=dc):
                edge_copy(-dr, -dc).wait_recv()

        at = (1 + dr) * 2
        merged = [
            jnp.where(
                lane % 4 < 2,
                nb[at, h * SUB : (h + 1) * SUB, :],
                nb[at + 1, h * SUB : (h + 1) * SUB, :],
            )
            for h in range(2)
        ]
        pairs = {
            0: [(r + 2, r) for r in range(rows)],
            -1: [(0, rows - 2), (1, rows - 1)],
            1: [(rows + 2, 0), (rows + 3, 1)],
        }[dr]
        for e, r in pairs:
            for g in range(all_groups):
                which, slot = (0, r * groups + g) if g < groups else (1, r)
                ext[e, g * SUB : (g + 1) * SUB, cols:wide] = pltpu.roll(
                    merged[which], (-(4 * slot + 2)) % LANES, 1
                )

    def rotate(src, left, right, first, last):
        def body(e, carry):
            for g in range(groups):
                at = pl.ds(g * SUB, SUB)
                v = src[e, at, :]
                left[e, at, :] = pltpu.roll(v, 1, 1)[:, : left.shape[2]]
                right[e, at, :] = pltpu.roll(v, wide - 1, 1)[:, : right.shape[2]]
            return carry

        lax.fori_loop(first, last, body, 0)

    def apply(srcs, dst, e_first, e_last, w_shift, dst_shift, lane_tiles):
        def body(t, carry):
            across = pl.ds(pl.multiple_of(t * LANES, LANES), LANES)
            window = {}

            def load(e):
                for g in range(groups):
                    for b, src in zip((-1, 0, 1), srcs):
                        window[e, g, b] = src[e, pl.ds(g * SUB, SUB), across]

            load(e_first - 1)
            load(e_first)
            for e in range(e_first, e_last):
                load(e + 1)
                taps = [
                    jnp.broadcast_to(ext[e + w_shift, pl.ds(n + k, 1), across], (SUB, LANES))
                    for k in range(SUB)
                ]
                degree = functools.reduce(jnp.add, taps)
                for g in range(groups):
                    total = degree * window[e, g, 0]
                    for k, (da, db) in enumerate(NEIGHBOURS):
                        total = total + taps[k] * window[e + da, g, db]
                    dst[e + dst_shift, pl.ds(g * SUB, SUB), across] = total
            return carry

        lax.fori_loop(0, lane_tiles, body, 0)

    wide_srcs = (ext_l, ext, ext_r)
    receive_edges(0, None)
    rotate(ext, ext_l, ext_r, 2, rows + 2)
    apply(wide_srcs, y1, 3, rows + 1, 0, -1, tiles + 1)
    receive_edges(-1, has_up)
    receive_edges(1, has_down)

    @pl.when(has_up)
    def _():
        row_copy(True).wait_recv()

    @pl.when(has_down)
    def _():
        row_copy(False).wait_recv()

    rotate(ext, ext_l, ext_r, 0, 2)
    rotate(ext, ext_l, ext_r, rows + 2, rows + 4)
    apply(wide_srcs, y1, 1, 3, 0, -1, tiles + 1)
    apply(wide_srcs, y1, rows + 1, rows + 3, 0, -1, tiles + 1)

    scale = 1.0 / (rows * cols * R * C)

    def gram(load):
        total = jnp.zeros((2 * n, 2 * n), jnp.float32)
        for r in range(rows):
            both = jnp.concatenate(split(load(r)), axis=0)
            total = total + lax.dot_general(both, both, NT, preferred_element_type=jnp.float32)
        half = total[0:n] + total[n : 2 * n]
        square = (half[:, 0:n] + half[:, n : 2 * n]) * scale
        return jnp.concatenate([square[g * SUB : (g + 1) * SUB] for g in range(groups)], axis=1)

    def gather_copies(which, axis, receiving):
        held, me, count, send_sems, recv_sems = (
            (held_row, i, R, gr_send, gr_recv) if axis == "row" else (held_col, j, C, gc_send, gc_recv)
        )
        at = which * 2 + (0 if axis == "row" else 1)
        copies = []
        for d in range(1, count):
            peer = lax.rem(me + d, count)
            slot = peer if receiving else me
            copies.append(pltpu.make_async_remote_copy(
                src_ref=sent.at[at], dst_ref=held.at[which, slot],
                send_sem=send_sems.at[which, d - 1], recv_sem=recv_sems.at[which, slot],
                device_id={"row": peer, "col": j} if axis == "row" else {"row": i, "col": peer},
                device_id_type=MESH,
            ))
        return copies

    def spread(which, axis, value):
        sent[which * 2 + (0 if axis == "row" else 1)] = value
        if axis == "row":
            held_row[which, i] = value
        else:
            held_col[which, j] = value
        for copy in gather_copies(which, axis, False):
            copy.start()

    def collect(which, axis):
        for copy in gather_copies(which, axis, True):
            copy.wait_recv()
        held, count = (held_row, R) if axis == "row" else (held_col, C)
        total = held[which, 0]
        for at in range(1, count):
            total = total + held[which, at]
        return total

    sub = lax.broadcasted_iota(jnp.int32, (SUB, LANES), 0)

    def eliminate(tile, step=4):
        blocks = []
        for g in range(groups):
            mine = tile if g == 0 else pltpu.roll(tile, LANES - g * n, 1)
            eye = (lane - n == sub + g * SUB).astype(jnp.float32)
            blocks.append(jnp.where(lane < n, mine, eye))
        for p in range(0, n, step):
            home, base = p // SUB, p % SUB
            line = [
                jnp.broadcast_to(blocks[home][base + q : base + q + 1, :], (SUB, LANES))
                for q in range(step)
            ]
            column = {
                (s, g): jnp.broadcast_to(blocks[g][:, p + s : p + s + 1], (SUB, LANES))
                for g in range(home, groups)
                for s in range(step)
            }
            corner = {
                (q, s): jnp.broadcast_to(column[s, home][base + q : base + q + 1, :], (SUB, LANES))
                for q in range(step)
                for s in range(q, step)
            }
            scaled = []
            for q in range(step):
                over = 1.0 / corner[q, q]
                scaled.append(line[q] * over)
                ratio = {s: corner[q, s] * over for s in range(q + 1, step)}
                for s in range(q + 1, step):
                    line[s] = line[s] - ratio[s] * line[q]
                    for t in range(s, step):
                        corner[s, t] = corner[s, t] - ratio[s] * corner[q, t]
                    for g in range(home, groups):
                        column[s, g] = column[s, g] - ratio[s] * column[q, g]
            for g in range(home, groups):
                if g == home and base + step == SUB:
                    continue
                update = column[0, g] * scaled[0]
                for q in range(1, step):
                    update = update + column[q, g] * scaled[q]
                if g == home:
                    update = jnp.where(sub >= base + step, update, 0.0)
                blocks[g] = blocks[g] - update
            for q in range(step):
                done = line[q] * (1.0 / jnp.sqrt(corner[q, q]))
                blocks[home] = jnp.where(sub == base + q, done, blocks[home])
        return jnp.concatenate(blocks, axis=0)

    spread(0, "row", gram(lambda r: y1[r + 1, :, 0:cols]))
    rotate(y1, y1_l, y1_r, 0, rows + 2)
    apply((y1_l, y1, y1_r), y2, 1, rows + 1, 1, -1, tiles)
    second = gram(lambda r: y2[r])
    spread(1, "row", second)
    spread(0, "col", collect(0, "row"))
    spread(1, "col", collect(1, "row"))
    table_1 = eliminate(collect(0, "col"))
    table_2 = eliminate(collect(1, "col"))

    inverse_1 = table_1[:, n : 2 * n]
    upper_2 = table_2[:, 0:n]
    inverse_2 = table_2[:, n : 2 * n]
    row_at = lax.broadcasted_iota(jnp.int32, (n, n), 0)
    col_at = lax.broadcasted_iota(jnp.int32, (n, n), 1)
    upper_2 = jnp.where(col_at >= row_at, upper_2, 0.0)
    last = lax.dot_general(
        upper_2, inverse_1, NT, precision=HIGHEST, preferred_element_type=jnp.float32
    )
    fac_ref[...] = jnp.where(col_at >= row_at, last, 0.0)

    inv_hi, inv_lo = split(inverse_2)
    left = jnp.concatenate([inv_hi, inv_lo, inv_hi], axis=1)
    stores = []
    for t0 in range(0, tiles, 2):
        for r in range(rows):
            hi, lo = split(y2[r, :, t0 * LANES : (t0 + 2) * LANES])
            right = jnp.concatenate([hi, hi, lo], axis=0)
            solved = jnp.dot(left, right, preferred_element_type=jnp.float32)
            for t in range(2):
                for g in range(groups):
                    staged[t0 + t, pl.ds(g * SUB * rows + r, SUB, stride=rows), :] = solved[
                        g * SUB : (g + 1) * SUB, t * LANES : (t + 1) * LANES
                    ]
        for t in range(t0, t0 + 2):
            stores.append(pltpu.make_async_copy(
                staged.at[t], out_ref.at[:, pl.ds(t * LANES, LANES)], store_sem.at[t]
            ))
            stores[-1].start()
    for store in stores:
        store.wait()

    for dr, ok_r in ups:
        for dc, ok_c in sides:
            @pl.when(cond(ok_r, ok_c))
            def _(dr=dr, dc=dc):
                edge_copy(dr, dc).wait_send()

    @pl.when(has_down)
    def _():
        row_copy(True).wait_send()

    @pl.when(has_up)
    def _():
        row_copy(False).wait_send()

    for which in range(2):
        for axis in ("row", "col"):
            for copy in gather_copies(which, axis, False):
                copy.wait_send()


def on_device(sketch, weights):
    n, rows, cols = sketch.shape
    R, C = lax.axis_size("row"), lax.axis_size("col")
    dma = pltpu.SemaphoreType.DMA
    f32 = jnp.float32
    basis, factor = pl.pallas_call(
        functools.partial(kernel, n, rows, cols, R, C),
        out_shape=(
            jax.ShapeDtypeStruct((n * rows, cols), f32),
            jax.ShapeDtypeStruct((n, n), f32),
        ),
        in_specs=[pl.BlockSpec(memory_space=pltpu.HBM)] * 2,
        out_specs=(
            pl.BlockSpec(memory_space=pl.ANY),
            pl.BlockSpec(memory_space=pltpu.VMEM),
        ),
        scratch_shapes=[
            pltpu.VMEM((cols // LANES, n * rows, LANES), f32),
            pltpu.VMEM((cols // LANES, SUB * rows, LANES), f32),
            pltpu.VMEM((cols // LANES, n * rows, LANES), f32),
            pltpu.VMEM((rows + 4, n + SUB, cols + LANES), f32),
            pltpu.VMEM((rows + 4, n, cols + LANES), f32),
            pltpu.VMEM((rows + 4, n, cols + LANES), f32),
            pltpu.VMEM((rows + 2, n, cols + LANES), f32),
            pltpu.VMEM((rows + 2, n, cols), f32),
            pltpu.VMEM((rows + 2, n, cols), f32),
            pltpu.VMEM((rows, n, cols), f32),
            pltpu.VMEM((2 * SUB, LANES), f32),
            pltpu.VMEM((6, 2 * SUB, LANES), f32),
            pltpu.VMEM((2, R, SUB, LANES), f32),
            pltpu.VMEM((2, C, SUB, LANES), f32),
            pltpu.VMEM((4, SUB, LANES), f32),
            dma((2, cols // LANES)), dma((cols // LANES,)), dma((2,)), dma((2,)), dma((6,)), dma((6,)),
            dma((2, R)), dma((2, R)), dma((2, C)), dma((2, C)),
        ],
        compiler_params=pltpu.CompilerParams(
            collective_id=0, has_side_effects=True, vmem_limit_bytes=32 * 1024 * 1024
        ),
    )(sketch.reshape(n * rows, cols), weights.reshape(SUB * rows, cols))
    return basis.reshape(n, rows, cols), factor


def solution(mesh):
    return jax.shard_map(
        on_device,
        mesh=mesh,
        in_specs=(P(None, ("sec", "row"), "col"), P(None, ("sec", "row"), "col")),
        out_specs=(P(None, ("sec", "row"), "col"), P("sec", None)),
        check_vma=False,
    )
```

```python
import functools

import jax
import jax.numpy as jnp
from jax import lax
from jax.experimental import pallas as pl
from jax.experimental.pallas import tpu as pltpu
from jax.sharding import PartitionSpec as P

LANES = 128
SUB = 8
NEIGHBOURS = ((-1, -1), (-1, 0), (-1, 1), (0, -1), (0, 1), (1, -1), (1, 0), (1, 1))
MESH = pl.DeviceIdType.MESH
NT = (((1,), (1,)), ((), ()))
HIGHEST = lax.Precision.HIGHEST


def split(x):
    hi = x.astype(jnp.bfloat16)
    lo = (x - hi.astype(jnp.float32)).astype(jnp.bfloat16)
    return hi, lo


def kernel(
    n, rows, cols, R, C, stages,
    sk_hbm, w_hbm, out_ref, fac_ref,
    raw, wraw, staged, ext, ext_l, ext_r, y1, y1_l, y1_r, y2, pack, nb, held, sent,
    load_sem, store_sem, row_send, row_recv, nb_send, nb_recv, gather_send, gather_recv,
):
    groups = n // SUB
    all_groups = groups + 1
    wide = cols + LANES
    i = lax.axis_index("row")
    j = lax.axis_index("col")
    has_up, has_down = i > 0, i < R - 1
    has_left, has_right = j > 0, j < C - 1

    tiles = cols // LANES
    loads = []
    for t in range(tiles):
        across = pl.ds(t * LANES, LANES)
        loads.append(pltpu.make_async_copy(sk_hbm.at[:, across], raw.at[t], load_sem.at[0, t]))
        loads.append(pltpu.make_async_copy(w_hbm.at[:, across], wraw.at[t], load_sem.at[1, t]))
    for load in loads:
        load.start()

    barrier = pltpu.get_barrier_semaphore()
    if len(stages) == 1:
        peers = [lax.rem(i * C + j + d, R * C) for d in range(1, R * C)]
        partners = [(lax.div(peer, C), lax.rem(peer, C)) for peer in peers]
    else:
        partners = [(lax.rem(i + d, R), j) for d in range(1, R)]
        partners += [(i, lax.rem(j + d, C)) for d in range(1, C)]
    for r, c in partners:
        pl.semaphore_signal(barrier, inc=1, device_id={"row": r, "col": c}, device_id_type=MESH)
    ups = ((-1, has_up), (0, None), (1, has_down))
    sides = ((-1, has_left), (1, has_right))
    for dr, ok_r in ups:
        for dc, ok_c in sides:
            if dr != 0 and len(stages) > 1:
                @pl.when(jnp.logical_and(ok_r, ok_c))
                def _(dr=dr, dc=dc):
                    pl.semaphore_signal(
                        barrier, inc=1, device_id={"row": i + dr, "col": j + dc},
                        device_id_type=MESH,
                    )
    diagonals = 0 if len(stages) == 1 else (has_up.astype(jnp.int32) + has_down.astype(jnp.int32)) * (
        has_left.astype(jnp.int32) + has_right.astype(jnp.int32)
    )

    lane = lax.broadcasted_iota(jnp.int32, (SUB, LANES), 1)

    def relayout(r):
        for t in range(tiles):
            across = slice(t * LANES, (t + 1) * LANES)
            for g in range(groups):
                ext[r + 2, g * SUB : (g + 1) * SUB, across] = raw[
                    t, pl.ds(g * SUB * rows + r, SUB, stride=rows), :
                ]
            ext[r + 2, n : n + SUB, across] = wraw[t, pl.ds(r, SUB, stride=rows), :]

    for load in loads:
        load.wait()
    for r in range(rows):
        relayout(r)

    def edge_copy(dr, dc):
        at = (1 - dr) * 2 + (0 if dc > 0 else 1)
        return pltpu.make_async_remote_copy(
            src_ref=pack, dst_ref=nb.at[at], send_sem=nb_send.at[at], recv_sem=nb_recv.at[at],
            device_id={"row": i + dr, "col": j + dc}, device_id_type=MESH,
        )

    def cond(*terms):
        terms = [t for t in terms if t is not None]
        return functools.reduce(jnp.logical_and, terms)

    def row_copy(down):
        src = rows if down else 2
        dst = 0 if down else rows + 2
        at = 0 if down else 1
        return pltpu.make_async_remote_copy(
            src_ref=ext.at[pl.ds(src, 2), :, pl.ds(0, cols)],
            dst_ref=ext.at[pl.ds(dst, 2), :, pl.ds(0, cols)],
            send_sem=row_send.at[at], recv_sem=row_recv.at[at],
            device_id={"row": i + (1 if down else -1), "col": j}, device_id_type=MESH,
        )

    pl.semaphore_wait(barrier, len(partners) + diagonals)

    @pl.when(has_down)
    def _():
        row_copy(True).start()

    @pl.when(has_up)
    def _():
        row_copy(False).start()

    packed = [jnp.zeros((SUB, LANES), jnp.float32), jnp.zeros((SUB, LANES), jnp.float32)]
    for r in range(rows):
        for g in range(all_groups):
            which, slot = (0, r * groups + g) if g < groups else (1, r)
            edge = jnp.where(
                lane < LANES // 2,
                ext[r + 2, g * SUB : (g + 1) * SUB, 0:LANES],
                ext[r + 2, g * SUB : (g + 1) * SUB, cols - LANES : cols],
            )
            moved = pltpu.roll(edge, (4 * slot + 2) % LANES, 1)
            packed[which] = jnp.where(lane // 4 == slot, moved, packed[which])
    pack[0:SUB, :] = packed[0]
    pack[SUB : 2 * SUB, :] = packed[1]

    for dr, ok_r in (ups[1], ups[0], ups[2]):
        for dc, ok_c in sides:
            @pl.when(cond(ok_r, ok_c))
            def _(dr=dr, dc=dc):
                edge_copy(dr, dc).start()

    @pl.when(jnp.logical_not(has_up))
    def _():
        ext[0:2, :, 0:cols] = jnp.zeros((2, n + SUB, cols), jnp.float32)

    @pl.when(jnp.logical_not(has_down))
    def _():
        ext[rows + 2 : rows + 4, :, 0:cols] = jnp.zeros((2, n + SUB, cols), jnp.float32)

    def receive_edges(dr, ok_r):
        for dc, ok_c in sides:
            at = (1 + dr) * 2 + (1 if dc > 0 else 0)
            ok = cond(ok_r, ok_c)

            @pl.when(jnp.logical_not(ok))
            def _(at=at):
                nb[at] = jnp.zeros((2 * SUB, LANES), jnp.float32)

            @pl.when(ok)
            def _(dr=dr, dc=dc):
                edge_copy(-dr, -dc).wait_recv()

        at = (1 + dr) * 2
        merged = [
            jnp.where(
                lane % 4 < 2,
                nb[at, h * SUB : (h + 1) * SUB, :],
                nb[at + 1, h * SUB : (h + 1) * SUB, :],
            )
            for h in range(2)
        ]
        pairs = {
            0: [(r + 2, r) for r in range(rows)],
            -1: [(0, rows - 2), (1, rows - 1)],
            1: [(rows + 2, 0), (rows + 3, 1)],
        }[dr]
        for e, r in pairs:
            for g in range(all_groups):
                which, slot = (0, r * groups + g) if g < groups else (1, r)
                ext[e, g * SUB : (g + 1) * SUB, cols:wide] = pltpu.roll(
                    merged[which], (-(4 * slot + 2)) % LANES, 1
                )

    def rotate(src, left, right, first, last):
        def body(e, carry):
            for g in range(groups):
                at = pl.ds(g * SUB, SUB)
                v = src[e, at, :]
                left[e, at, :] = pltpu.roll(v, 1, 1)[:, : left.shape[2]]
                right[e, at, :] = pltpu.roll(v, wide - 1, 1)[:, : right.shape[2]]
            return carry

        lax.fori_loop(first, last, body, 0)

    def apply(srcs, dst, e_first, e_last, w_shift, dst_shift, lane_tiles):
        def body(t, carry):
            across = pl.ds(pl.multiple_of(t * LANES, LANES), LANES)
            window = {}

            def load(e):
                for g in range(groups):
                    for b, src in zip((-1, 0, 1), srcs):
                        window[e, g, b] = src[e, pl.ds(g * SUB, SUB), across]

            load(e_first - 1)
            load(e_first)
            for e in range(e_first, e_last):
                load(e + 1)
                taps = [
                    jnp.broadcast_to(ext[e + w_shift, pl.ds(n + k, 1), across], (SUB, LANES))
                    for k in range(SUB)
                ]
                degree = functools.reduce(jnp.add, taps)
                for g in range(groups):
                    total = degree * window[e, g, 0]
                    for k, (da, db) in enumerate(NEIGHBOURS):
                        total = total + taps[k] * window[e + da, g, db]
                    dst[e + dst_shift, pl.ds(g * SUB, SUB), across] = total
            return carry

        lax.fori_loop(0, lane_tiles, body, 0)

    wide_srcs = (ext_l, ext, ext_r)
    receive_edges(0, None)
    rotate(ext, ext_l, ext_r, 2, rows + 2)
    apply(wide_srcs, y1, 3, rows + 1, 0, -1, tiles + 1)
    receive_edges(-1, has_up)
    receive_edges(1, has_down)

    @pl.when(has_up)
    def _():
        row_copy(True).wait_recv()

    @pl.when(has_down)
    def _():
        row_copy(False).wait_recv()

    rotate(ext, ext_l, ext_r, 0, 2)
    rotate(ext, ext_l, ext_r, rows + 2, rows + 4)
    apply(wide_srcs, y1, 1, 3, 0, -1, tiles + 1)
    apply(wide_srcs, y1, rows + 1, rows + 3, 0, -1, tiles + 1)

    scale = 1.0 / (rows * cols * R * C)

    def gram(load):
        total = jnp.zeros((2 * n, 2 * n), jnp.float32)
        for r in range(rows):
            both = jnp.concatenate(split(load(r)), axis=0)
            total = total + lax.dot_general(both, both, NT, preferred_element_type=jnp.float32)
        half = total[0:n] + total[n : 2 * n]
        square = (half[:, 0:n] + half[:, n : 2 * n]) * scale
        return jnp.concatenate([square[g * SUB : (g + 1) * SUB] for g in range(groups)], axis=1)

    def gather_copies(which, stage, receiving):
        axes, count = stages[stage]
        me = {"row": i, "col": j, "both": i * C + j}[axes]
        copies = []
        for d in range(1, count):
            peer = lax.rem(me + d, count)
            slot = peer if receiving else me
            target = {
                "row": {"row": peer, "col": j},
                "col": {"row": i, "col": peer},
                "both": {"row": lax.div(peer, C), "col": lax.rem(peer, C)},
            }[axes]
            copies.append(pltpu.make_async_remote_copy(
                src_ref=sent.at[which, stage], dst_ref=held.at[which, stage, slot],
                send_sem=gather_send.at[which, stage, d - 1],
                recv_sem=gather_recv.at[which, stage, slot],
                device_id=target, device_id_type=MESH,
            ))
        return copies

    def spread(which, stage, value):
        axes, count = stages[stage]
        me = {"row": i, "col": j, "both": i * C + j}[axes]
        sent[which, stage] = value
        held[which, stage, me] = value
        for copy in gather_copies(which, stage, False):
            copy.start()

    def collect(which, stage):
        for copy in gather_copies(which, stage, True):
            copy.wait_recv()
        terms = [held[which, stage, at] for at in range(stages[stage][1])]
        while len(terms) > 1:
            terms = [sum(terms[k + 1 : k + 2], terms[k]) for k in range(0, len(terms), 2)]
        return terms[0]

    sub = lax.broadcasted_iota(jnp.int32, (SUB, LANES), 0)

    def eliminate(tile, step=4):
        blocks = []
        for g in range(groups):
            mine = tile if g == 0 else pltpu.roll(tile, LANES - g * n, 1)
            eye = (lane - n == sub + g * SUB).astype(jnp.float32)
            blocks.append(jnp.where(lane < n, mine, eye))
        for p in range(0, n, step):
            home, base = p // SUB, p % SUB
            line = [
                jnp.broadcast_to(blocks[home][base + q : base + q + 1, :], (SUB, LANES))
                for q in range(step)
            ]
            column = {
                (s, g): jnp.broadcast_to(blocks[g][:, p + s : p + s + 1], (SUB, LANES))
                for g in range(home, groups)
                for s in range(step)
            }
            corner = {
                (q, s): jnp.broadcast_to(column[s, home][base + q : base + q + 1, :], (SUB, LANES))
                for q in range(step)
                for s in range(q, step)
            }
            scaled = []
            for q in range(step):
                over = 1.0 / corner[q, q]
                scaled.append(line[q] * over)
                ratio = {s: corner[q, s] * over for s in range(q + 1, step)}
                for s in range(q + 1, step):
                    line[s] = line[s] - ratio[s] * line[q]
                    for t in range(s, step):
                        corner[s, t] = corner[s, t] - ratio[s] * corner[q, t]
                    for g in range(home, groups):
                        column[s, g] = column[s, g] - ratio[s] * column[q, g]
            for g in range(home, groups):
                if g == home and base + step == SUB:
                    continue
                update = column[0, g] * scaled[0]
                for q in range(1, step):
                    update = update + column[q, g] * scaled[q]
                if g == home:
                    update = jnp.where(sub >= base + step, update, 0.0)
                blocks[g] = blocks[g] - update
            for q in range(step):
                done = line[q] * (1.0 / jnp.sqrt(corner[q, q]))
                blocks[home] = jnp.where(sub == base + q, done, blocks[home])
        return jnp.concatenate(blocks, axis=0)

    spread(0, 0, gram(lambda r: y1[r + 1, :, 0:cols]))
    rotate(y1, y1_l, y1_r, 0, rows + 2)
    apply((y1_l, y1, y1_r), y2, 1, rows + 1, 1, -1, tiles)
    spread(1, 0, gram(lambda r: y2[r]))
    for stage in range(1, len(stages)):
        spread(0, stage, collect(0, stage - 1))
        spread(1, stage, collect(1, stage - 1))
    table_1 = eliminate(collect(0, len(stages) - 1))
    table_2 = eliminate(collect(1, len(stages) - 1))

    inverse_1 = table_1[:, n : 2 * n]
    upper_2 = table_2[:, 0:n]
    inverse_2 = table_2[:, n : 2 * n]
    row_at = lax.broadcasted_iota(jnp.int32, (n, n), 0)
    col_at = lax.broadcasted_iota(jnp.int32, (n, n), 1)
    upper_2 = jnp.where(col_at >= row_at, upper_2, 0.0)
    last = lax.dot_general(
        upper_2, inverse_1, NT, precision=HIGHEST, preferred_element_type=jnp.float32
    )
    fac_ref[...] = jnp.where(col_at >= row_at, last, 0.0)

    inv_hi, inv_lo = split(inverse_2)
    left = jnp.concatenate([inv_hi, inv_lo, inv_hi], axis=1)
    stores = []
    for t0 in range(0, tiles, 2):
        for r in range(rows):
            hi, lo = split(y2[r, :, t0 * LANES : (t0 + 2) * LANES])
            right = jnp.concatenate([hi, hi, lo], axis=0)
            solved = jnp.dot(left, right, preferred_element_type=jnp.float32)
            for t in range(2):
                for g in range(groups):
                    staged[t0 + t, pl.ds(g * SUB * rows + r, SUB, stride=rows), :] = solved[
                        g * SUB : (g + 1) * SUB, t * LANES : (t + 1) * LANES
                    ]
        for t in range(t0, t0 + 2):
            stores.append(pltpu.make_async_copy(
                staged.at[t], out_ref.at[:, pl.ds(t * LANES, LANES)], store_sem.at[t]
            ))
            stores[-1].start()
    for store in stores:
        store.wait()

    for dr, ok_r in ups:
        for dc, ok_c in sides:
            @pl.when(cond(ok_r, ok_c))
            def _(dr=dr, dc=dc):
                edge_copy(dr, dc).wait_send()

    @pl.when(has_down)
    def _():
        row_copy(True).wait_send()

    @pl.when(has_up)
    def _():
        row_copy(False).wait_send()

    for which in range(2):
        for stage in range(len(stages)):
            for copy in gather_copies(which, stage, False):
                copy.wait_send()


def on_device(sketch, weights):
    n, rows, cols = sketch.shape
    R, C = lax.axis_size("row"), lax.axis_size("col")
    stages = (("both", R * C),) if R * C <= 16 else (("row", R), ("col", C))
    peers = max(count for _, count in stages)
    dma = pltpu.SemaphoreType.DMA
    f32 = jnp.float32
    basis, factor = pl.pallas_call(
        functools.partial(kernel, n, rows, cols, R, C, stages),
        out_shape=(
            jax.ShapeDtypeStruct((n * rows, cols), f32),
            jax.ShapeDtypeStruct((n, n), f32),
        ),
        in_specs=[pl.BlockSpec(memory_space=pltpu.HBM)] * 2,
        out_specs=(
            pl.BlockSpec(memory_space=pl.ANY),
            pl.BlockSpec(memory_space=pltpu.VMEM),
        ),
        scratch_shapes=[
            pltpu.VMEM((cols // LANES, n * rows, LANES), f32),
            pltpu.VMEM((cols // LANES, SUB * rows, LANES), f32),
            pltpu.VMEM((cols // LANES, n * rows, LANES), f32),
            pltpu.VMEM((rows + 4, n + SUB, cols + LANES), f32),
            pltpu.VMEM((rows + 4, n, cols + LANES), f32),
            pltpu.VMEM((rows + 4, n, cols + LANES), f32),
            pltpu.VMEM((rows + 2, n, cols + LANES), f32),
            pltpu.VMEM((rows + 2, n, cols), f32),
            pltpu.VMEM((rows + 2, n, cols), f32),
            pltpu.VMEM((rows, n, cols), f32),
            pltpu.VMEM((2 * SUB, LANES), f32),
            pltpu.VMEM((6, 2 * SUB, LANES), f32),
            pltpu.VMEM((2, len(stages), peers, SUB, LANES), f32),
            pltpu.VMEM((2, len(stages), SUB, LANES), f32),
            dma((2, cols // LANES)), dma((cols // LANES,)), dma((2,)), dma((2,)), dma((6,)), dma((6,)),
            dma((2, len(stages), peers)), dma((2, len(stages), peers)),
        ],
        compiler_params=pltpu.CompilerParams(
            collective_id=0, has_side_effects=True, vmem_limit_bytes=32 * 1024 * 1024
        ),
    )(sketch.reshape(n * rows, cols), weights.reshape(SUB * rows, cols))
    return basis.reshape(n, rows, cols), factor


def solution(mesh):
    return jax.shard_map(
        on_device,
        mesh=mesh,
        in_specs=(P(None, ("sec", "row"), "col"), P(None, ("sec", "row"), "col")),
        out_specs=(P(None, ("sec", "row"), "col"), P("sec", None)),
        check_vma=False,
    )
```

```python
import functools

import jax
import jax.numpy as jnp
from jax import lax
from jax.experimental import pallas as pl
from jax.experimental.pallas import tpu as pltpu
from jax.sharding import PartitionSpec as P

LANES = 128
SUB = 8
NEIGHBOURS = ((-1, -1), (-1, 0), (-1, 1), (0, -1), (0, 1), (1, -1), (1, 0), (1, 1))
MESH = pl.DeviceIdType.MESH
NT = (((1,), (1,)), ((), ()))
HIGHEST = lax.Precision.HIGHEST


def split(x):
    hi = x.astype(jnp.bfloat16)
    lo = (x - hi.astype(jnp.float32)).astype(jnp.bfloat16)
    return hi, lo


def kernel(
    n, rows, cols, R, C, stages,
    sk_hbm, w_hbm, y2, tables,
    raw, wraw, ext, ext_l, ext_r, y1, y1_l, y1_r, pack, nb, held, sent,
    load_sem, row_send, row_recv, nb_send, nb_recv, gather_send, gather_recv,
):
    groups = n // SUB
    all_groups = groups + 1
    wide = cols + LANES
    i = lax.axis_index("row")
    j = lax.axis_index("col")
    has_up, has_down = i > 0, i < R - 1
    has_left, has_right = j > 0, j < C - 1

    tiles = cols // LANES
    loads = []
    for t in range(tiles):
        across = pl.ds(t * LANES, LANES)
        loads.append(pltpu.make_async_copy(sk_hbm.at[:, across], raw.at[t], load_sem.at[0, t]))
        loads.append(pltpu.make_async_copy(w_hbm.at[:, across], wraw.at[t], load_sem.at[1, t]))
    for load in loads:
        load.start()

    barrier = pltpu.get_barrier_semaphore()
    if len(stages) == 1:
        peers = [lax.rem(i * C + j + d, R * C) for d in range(1, R * C)]
        partners = [(lax.div(peer, C), lax.rem(peer, C)) for peer in peers]
    else:
        partners = [(lax.rem(i + d, R), j) for d in range(1, R)]
        partners += [(i, lax.rem(j + d, C)) for d in range(1, C)]
    for r, c in partners:
        pl.semaphore_signal(barrier, inc=1, device_id={"row": r, "col": c}, device_id_type=MESH)
    ups = ((-1, has_up), (0, None), (1, has_down))
    sides = ((-1, has_left), (1, has_right))
    for dr, ok_r in ups:
        for dc, ok_c in sides:
            if dr != 0 and len(stages) > 1:
                @pl.when(jnp.logical_and(ok_r, ok_c))
                def _(dr=dr, dc=dc):
                    pl.semaphore_signal(
                        barrier, inc=1, device_id={"row": i + dr, "col": j + dc},
                        device_id_type=MESH,
                    )
    diagonals = 0 if len(stages) == 1 else (has_up.astype(jnp.int32) + has_down.astype(jnp.int32)) * (
        has_left.astype(jnp.int32) + has_right.astype(jnp.int32)
    )

    lane = lax.broadcasted_iota(jnp.int32, (SUB, LANES), 1)

    def relayout(r):
        for t in range(tiles):
            across = slice(t * LANES, (t + 1) * LANES)
            for g in range(groups):
                ext[r + 2, g * SUB : (g + 1) * SUB, across] = raw[
                    t, pl.ds(g * SUB * rows + r, SUB, stride=rows), :
                ]
            ext[r + 2, n : n + SUB, across] = wraw[t, pl.ds(r, SUB, stride=rows), :]

    for load in loads:
        load.wait()
    for r in range(rows):
        relayout(r)

    def edge_copy(dr, dc):
        at = (1 - dr) * 2 + (0 if dc > 0 else 1)
        return pltpu.make_async_remote_copy(
            src_ref=pack, dst_ref=nb.at[at], send_sem=nb_send.at[at], recv_sem=nb_recv.at[at],
            device_id={"row": i + dr, "col": j + dc}, device_id_type=MESH,
        )

    def cond(*terms):
        terms = [t for t in terms if t is not None]
        return functools.reduce(jnp.logical_and, terms)

    def row_copy(down):
        src = rows if down else 2
        dst = 0 if down else rows + 2
        at = 0 if down else 1
        return pltpu.make_async_remote_copy(
            src_ref=ext.at[pl.ds(src, 2), :, pl.ds(0, cols)],
            dst_ref=ext.at[pl.ds(dst, 2), :, pl.ds(0, cols)],
            send_sem=row_send.at[at], recv_sem=row_recv.at[at],
            device_id={"row": i + (1 if down else -1), "col": j}, device_id_type=MESH,
        )

    pl.semaphore_wait(barrier, len(partners) + diagonals)

    @pl.when(has_down)
    def _():
        row_copy(True).start()

    @pl.when(has_up)
    def _():
        row_copy(False).start()

    packed = [jnp.zeros((SUB, LANES), jnp.float32), jnp.zeros((SUB, LANES), jnp.float32)]
    for r in range(rows):
        for g in range(all_groups):
            which, slot = (0, r * groups + g) if g < groups else (1, r)
            edge = jnp.where(
                lane < LANES // 2,
                ext[r + 2, g * SUB : (g + 1) * SUB, 0:LANES],
                ext[r + 2, g * SUB : (g + 1) * SUB, cols - LANES : cols],
            )
            moved = pltpu.roll(edge, (4 * slot + 2) % LANES, 1)
            packed[which] = jnp.where(lane // 4 == slot, moved, packed[which])
    pack[0:SUB, :] = packed[0]
    pack[SUB : 2 * SUB, :] = packed[1]

    for dr, ok_r in (ups[1], ups[0], ups[2]):
        for dc, ok_c in sides:
            @pl.when(cond(ok_r, ok_c))
            def _(dr=dr, dc=dc):
                edge_copy(dr, dc).start()

    @pl.when(jnp.logical_not(has_up))
    def _():
        ext[0:2, :, 0:cols] = jnp.zeros((2, n + SUB, cols), jnp.float32)

    @pl.when(jnp.logical_not(has_down))
    def _():
        ext[rows + 2 : rows + 4, :, 0:cols] = jnp.zeros((2, n + SUB, cols), jnp.float32)

    def receive_edges(dr, ok_r):
        for dc, ok_c in sides:
            at = (1 + dr) * 2 + (1 if dc > 0 else 0)
            ok = cond(ok_r, ok_c)

            @pl.when(jnp.logical_not(ok))
            def _(at=at):
                nb[at] = jnp.zeros((2 * SUB, LANES), jnp.float32)

            @pl.when(ok)
            def _(dr=dr, dc=dc):
                edge_copy(-dr, -dc).wait_recv()

        at = (1 + dr) * 2
        merged = [
            jnp.where(
                lane % 4 < 2,
                nb[at, h * SUB : (h + 1) * SUB, :],
                nb[at + 1, h * SUB : (h + 1) * SUB, :],
            )
            for h in range(2)
        ]
        pairs = {
            0: [(r + 2, r) for r in range(rows)],
            -1: [(0, rows - 2), (1, rows - 1)],
            1: [(rows + 2, 0), (rows + 3, 1)],
        }[dr]
        for e, r in pairs:
            for g in range(all_groups):
                which, slot = (0, r * groups + g) if g < groups else (1, r)
                ext[e, g * SUB : (g + 1) * SUB, cols:wide] = pltpu.roll(
                    merged[which], (-(4 * slot + 2)) % LANES, 1
                )

    def rotate(src, left, right, first, last):
        def body(e, carry):
            for g in range(groups):
                at = pl.ds(g * SUB, SUB)
                v = src[e, at, :]
                left[e, at, :] = pltpu.roll(v, 1, 1)[:, : left.shape[2]]
                right[e, at, :] = pltpu.roll(v, wide - 1, 1)[:, : right.shape[2]]
            return carry

        lax.fori_loop(first, last, body, 0)

    def apply(srcs, dst, e_first, e_last, w_shift, dst_shift, lane_tiles):
        def body(t, carry):
            across = pl.ds(pl.multiple_of(t * LANES, LANES), LANES)
            window = {}

            def load(e):
                for g in range(groups):
                    for b, src in zip((-1, 0, 1), srcs):
                        window[e, g, b] = src[e, pl.ds(g * SUB, SUB), across]

            load(e_first - 1)
            load(e_first)
            for e in range(e_first, e_last):
                load(e + 1)
                taps = [
                    jnp.broadcast_to(ext[e + w_shift, pl.ds(n + k, 1), across], (SUB, LANES))
                    for k in range(SUB)
                ]
                degree = functools.reduce(jnp.add, taps)
                for g in range(groups):
                    total = degree * window[e, g, 0]
                    for k, (da, db) in enumerate(NEIGHBOURS):
                        total = total + taps[k] * window[e + da, g, db]
                    dst[e + dst_shift, pl.ds(g * SUB, SUB), across] = total
            return carry

        lax.fori_loop(0, lane_tiles, body, 0)

    wide_srcs = (ext_l, ext, ext_r)
    receive_edges(0, None)
    rotate(ext, ext_l, ext_r, 2, rows + 2)
    apply(wide_srcs, y1, 3, rows + 1, 0, -1, tiles + 1)
    receive_edges(-1, has_up)
    receive_edges(1, has_down)

    @pl.when(has_up)
    def _():
        row_copy(True).wait_recv()

    @pl.when(has_down)
    def _():
        row_copy(False).wait_recv()

    rotate(ext, ext_l, ext_r, 0, 2)
    rotate(ext, ext_l, ext_r, rows + 2, rows + 4)
    apply(wide_srcs, y1, 1, 3, 0, -1, tiles + 1)
    apply(wide_srcs, y1, rows + 1, rows + 3, 0, -1, tiles + 1)

    scale = 1.0 / (rows * cols * R * C)

    def gram(load):
        total = jnp.zeros((2 * n, 2 * n), jnp.float32)
        for r in range(rows):
            both = jnp.concatenate(split(load(r)), axis=0)
            total = total + lax.dot_general(both, both, NT, preferred_element_type=jnp.float32)
        half = total[0:n] + total[n : 2 * n]
        square = (half[:, 0:n] + half[:, n : 2 * n]) * scale
        return jnp.concatenate([square[g * SUB : (g + 1) * SUB] for g in range(groups)], axis=1)

    def gather_copies(which, stage, receiving):
        axes, count = stages[stage]
        me = {"row": i, "col": j, "both": i * C + j}[axes]
        copies = []
        for d in range(1, count):
            peer = lax.rem(me + d, count)
            slot = peer if receiving else me
            target = {
                "row": {"row": peer, "col": j},
                "col": {"row": i, "col": peer},
                "both": {"row": lax.div(peer, C), "col": lax.rem(peer, C)},
            }[axes]
            copies.append(pltpu.make_async_remote_copy(
                src_ref=sent.at[which, stage], dst_ref=held.at[which, stage, slot],
                send_sem=gather_send.at[which, stage, d - 1],
                recv_sem=gather_recv.at[which, stage, slot],
                device_id=target, device_id_type=MESH,
            ))
        return copies

    def spread(which, stage, value):
        axes, count = stages[stage]
        me = {"row": i, "col": j, "both": i * C + j}[axes]
        sent[which, stage] = value
        held[which, stage, me] = value
        for copy in gather_copies(which, stage, False):
            copy.start()

    def collect(which, stage):
        for copy in gather_copies(which, stage, True):
            copy.wait_recv()
        terms = [held[which, stage, at] for at in range(stages[stage][1])]
        while len(terms) > 1:
            terms = [sum(terms[k + 1 : k + 2], terms[k]) for k in range(0, len(terms), 2)]
        return terms[0]

    sub = lax.broadcasted_iota(jnp.int32, (SUB, LANES), 0)

    def eliminate(tile, step=4):
        blocks = []
        for g in range(groups):
            mine = tile if g == 0 else pltpu.roll(tile, LANES - g * n, 1)
            eye = (lane - n == sub + g * SUB).astype(jnp.float32)
            blocks.append(jnp.where(lane < n, mine, eye))
        for p in range(0, n, step):
            home, base = p // SUB, p % SUB
            line = [
                jnp.broadcast_to(blocks[home][base + q : base + q + 1, :], (SUB, LANES))
                for q in range(step)
            ]
            column = {
                (s, g): jnp.broadcast_to(blocks[g][:, p + s : p + s + 1], (SUB, LANES))
                for g in range(home, groups)
                for s in range(step)
            }
            corner = {
                (q, s): jnp.broadcast_to(column[s, home][base + q : base + q + 1, :], (SUB, LANES))
                for q in range(step)
                for s in range(q, step)
            }
            scaled = []
            for q in range(step):
                over = 1.0 / corner[q, q]
                scaled.append(line[q] * over)
                ratio = {s: corner[q, s] * over for s in range(q + 1, step)}
                for s in range(q + 1, step):
                    line[s] = line[s] - ratio[s] * line[q]
                    for t in range(s, step):
                        corner[s, t] = corner[s, t] - ratio[s] * corner[q, t]
                    for g in range(home, groups):
                        column[s, g] = column[s, g] - ratio[s] * column[q, g]
            for g in range(home, groups):
                if g == home and base + step == SUB:
                    continue
                update = column[0, g] * scaled[0]
                for q in range(1, step):
                    update = update + column[q, g] * scaled[q]
                if g == home:
                    update = jnp.where(sub >= base + step, update, 0.0)
                blocks[g] = blocks[g] - update
            for q in range(step):
                done = line[q] * (1.0 / jnp.sqrt(corner[q, q]))
                blocks[home] = jnp.where(sub == base + q, done, blocks[home])
        return jnp.concatenate(blocks, axis=0)

    spread(0, 0, gram(lambda r: y1[r + 1, :, 0:cols]))
    rotate(y1, y1_l, y1_r, 0, rows + 2)
    apply((y1_l, y1, y1_r), y2, 1, rows + 1, 1, -1, tiles)
    spread(1, 0, gram(lambda r: y2[r]))
    for stage in range(1, len(stages)):
        spread(0, stage, collect(0, stage - 1))
        spread(1, stage, collect(1, stage - 1))
    table_1 = eliminate(collect(0, len(stages) - 1))
    table_2 = eliminate(collect(1, len(stages) - 1))

    tables[0] = table_1
    tables[1] = table_2

    for dr, ok_r in ups:
        for dc, ok_c in sides:
            @pl.when(cond(ok_r, ok_c))
            def _(dr=dr, dc=dc):
                edge_copy(dr, dc).wait_send()

    @pl.when(has_down)
    def _():
        row_copy(True).wait_send()

    @pl.when(has_up)
    def _():
        row_copy(False).wait_send()

    for which in range(2):
        for stage in range(len(stages)):
            for copy in gather_copies(which, stage, False):
                copy.wait_send()


def finish(n, rows, cols, y2, tables, out_ref, fac_ref, staged, store_sem):
    groups = n // SUB
    tiles = cols // LANES
    inverse_1 = tables[0, :, n : 2 * n]
    upper_2 = tables[1, :, 0:n]
    inverse_2 = tables[1, :, n : 2 * n]
    row_at = lax.broadcasted_iota(jnp.int32, (n, n), 0)
    col_at = lax.broadcasted_iota(jnp.int32, (n, n), 1)
    upper_2 = jnp.where(col_at >= row_at, upper_2, 0.0)
    last = lax.dot_general(
        upper_2, inverse_1, NT, precision=HIGHEST, preferred_element_type=jnp.float32
    )
    fac_ref[...] = jnp.where(col_at >= row_at, last, 0.0)

    inv_hi, inv_lo = split(inverse_2)
    left = jnp.concatenate([inv_hi, inv_lo, inv_hi], axis=1)
    stores = []
    for t0 in range(0, tiles, 2):
        for r in range(rows):
            hi, lo = split(y2[r, :, t0 * LANES : (t0 + 2) * LANES])
            right = jnp.concatenate([hi, hi, lo], axis=0)
            solved = jnp.dot(left, right, preferred_element_type=jnp.float32)
            for t in range(2):
                for g in range(groups):
                    staged[t0 + t, pl.ds(g * SUB * rows + r, SUB, stride=rows), :] = solved[
                        g * SUB : (g + 1) * SUB, t * LANES : (t + 1) * LANES
                    ]
        for t in range(t0, t0 + 2):
            stores.append(pltpu.make_async_copy(
                staged.at[t], out_ref.at[:, pl.ds(t * LANES, LANES)], store_sem.at[t]
            ))
            stores[-1].start()
    for store in stores:
        store.wait()


def on_device(sketch, weights):
    n, rows, cols = sketch.shape
    R, C = lax.axis_size("row"), lax.axis_size("col")
    stages = (("both", R * C),) if R * C <= 16 else (("row", R), ("col", C))
    peers = max(count for _, count in stages)
    dma = pltpu.SemaphoreType.DMA
    f32 = jnp.float32
    image, tables = pl.pallas_call(
        functools.partial(kernel, n, rows, cols, R, C, stages),
        out_shape=(
            jax.ShapeDtypeStruct((rows, n, cols), f32),
            jax.ShapeDtypeStruct((2, n, LANES), f32),
        ),
        in_specs=[pl.BlockSpec(memory_space=pltpu.HBM)] * 2,
        out_specs=(
            pl.BlockSpec(memory_space=pltpu.VMEM),
            pl.BlockSpec(memory_space=pltpu.VMEM),
        ),
        scratch_shapes=[
            pltpu.VMEM((cols // LANES, n * rows, LANES), f32),
            pltpu.VMEM((cols // LANES, SUB * rows, LANES), f32),
            pltpu.VMEM((rows + 4, n + SUB, cols + LANES), f32),
            pltpu.VMEM((rows + 4, n, cols + LANES), f32),
            pltpu.VMEM((rows + 4, n, cols + LANES), f32),
            pltpu.VMEM((rows + 2, n, cols + LANES), f32),
            pltpu.VMEM((rows + 2, n, cols), f32),
            pltpu.VMEM((rows + 2, n, cols), f32),
            pltpu.VMEM((2 * SUB, LANES), f32),
            pltpu.VMEM((6, 2 * SUB, LANES), f32),
            pltpu.VMEM((2, len(stages), peers, SUB, LANES), f32),
            pltpu.VMEM((2, len(stages), SUB, LANES), f32),
            dma((2, cols // LANES)), dma((2,)), dma((2,)), dma((6,)), dma((6,)),
            dma((2, len(stages), peers)), dma((2, len(stages), peers)),
        ],
        compiler_params=pltpu.CompilerParams(
            collective_id=0, has_side_effects=True, vmem_limit_bytes=62 * 1024 * 1024
        ),
    )(sketch.reshape(n * rows, cols), weights.reshape(SUB * rows, cols))
    basis, factor = pl.pallas_call(
        functools.partial(finish, n, rows, cols),
        out_shape=(
            jax.ShapeDtypeStruct((n * rows, cols), f32),
            jax.ShapeDtypeStruct((n, n), f32),
        ),
        in_specs=[pl.BlockSpec(memory_space=pltpu.VMEM)] * 2,
        out_specs=(
            pl.BlockSpec(memory_space=pl.ANY),
            pl.BlockSpec(memory_space=pltpu.VMEM),
        ),
        scratch_shapes=[
            pltpu.VMEM((cols // LANES, n * rows, LANES), f32),
            dma((cols // LANES,)),
        ],
        compiler_params=pltpu.CompilerParams(vmem_limit_bytes=62 * 1024 * 1024),
    )(image, tables)
    return basis.reshape(n, rows, cols), factor


def solution(mesh):
    return jax.shard_map(
        on_device,
        mesh=mesh,
        in_specs=(P(None, ("sec", "row"), "col"), P(None, ("sec", "row"), "col")),
        out_specs=(P(None, ("sec", "row"), "col"), P("sec", None)),
        check_vma=False,
    )
```
